32 devices in a mesh: level: 2 (over y), lon: 8 (over z, x), lat: 2 (over core).
Axes of the slice: x: 2, y: 2, z: 4, core: 2. Of those that a mesh axis runs over, the one named last changes fastest.
Arguments:
- wind_snaps: float32 [4, 32, 32, 256], P('level', None, 'lon', 'lat'), parts along dimension 0, may hold values from -48 to 48
- old_basis: float32 [4, 64, 32, 256], P('level', None, 'lon', 'lat'), parts along dimension 0, may hold values from -17 to 17
- old_values: float32 [4, 64], P('level'), parts along dimension 0, may hold values from 1 to 4
Outputs:
- new_basis: float32 [4, 64, 32, 256], P('level', None, 'lon', 'lat'), parts along dimension 0
- new_values: float32 [4, 64], P('level'), parts along dimension 0
The draws below stay inside these ranges and needn't reach their ends.
There are 2 independent parts, one for each index of `level`. The reference program is written for one: setup_inputs(seed, part) draws one part's arguments, and reference() takes and returns one part's arrays. A program takes and returns all parts, laid end to end along the dimension named above; each array names one. Nothing has to cross between parts.
All inputs are finite; a program needn't handle non-finite values.
Results may differ from the reference program's by a relative error of at most 0.00012.
Values sent between devices are 32-bit elements; how exact they have to be, the bound alone decides.
A program may use at most 64 MiB of HBM per device.

```python
import math
import jax
import jax.numpy as jnp
from jax import lax

K = 64
S = 32
ITERS = 2
NLON = 32
NLAT = 256


def clipped_normal(key, shape):
    return jnp.clip(jax.random.normal(key, shape, jnp.float32), -4.0, 4.0)


def base_winds(key):
    shape = (2, K, NLON, NLAT)
    return clipped_normal(jax.random.fold_in(key, 11), shape)


def curl_fields(winds):
    row_place = jnp.arange(NLAT, dtype=jnp.float32)
    cosines = jnp.cos(((row_place + 0.5) / NLAT - 0.5) * (jnp.pi / 2.0))
    east_wind = winds[0]
    north_wind = winds[1]

    def lon_diff(values):
        return jnp.roll(values, -1, axis=1) - jnp.roll(values, 1, axis=1)

    def lat_diff(values):
        padded = jnp.pad(values * cosines, ((0, 0), (0, 0), (1, 1)))
        return padded[:, :, 2:] - padded[:, :, :-2]
    twice_cos = 2.0 * cosines
    vorticity = (lon_diff(north_wind) - lat_diff(east_wind)) / twice_cos
    divergence = (lon_diff(east_wind) + lat_diff(north_wind)) / twice_cos
    return jnp.stack([vorticity, divergence])


def draw_wind_snaps(key, part):
    base = base_winds(key)
    shape = (2, S, NLON, NLAT)
    noise = clipped_normal(jax.random.fold_in(key, 12), shape)
    mixed = base[:, :S] + 0.5 * base[:, S:2 * S] + 0.8 * noise
    lon_place = jnp.arange(NLON, dtype=jnp.float32)
    envelope = jnp.exp(jnp.log(3.0) * lon_place / NLON)
    return mixed * envelope[:, None]


def draw_old_basis(key, part):
    base = base_winds(key)
    fields = curl_fields(base)
    noise = clipped_normal(jax.random.fold_in(key, 13), (2, K, NLON, NLAT))
    shared = clipped_normal(jax.random.fold_in(key, 14), (2, 1, NLON, NLAT))
    return fields + 0.5 * noise + 0.8 * shared


def setup_inputs(seed: int = 0, part: int = 0) -> dict:
    key_of = jax.random.split(jax.random.key(seed), 4)
    part_splits = jax.random.split(jax.random.fold_in(key_of[3], part), 4)
    return {
        "wind_snaps": draw_wind_snaps(jax.random.fold_in(jax.random.fold_in(key_of[3], part), 71), part),
        "old_basis": draw_old_basis(jax.random.fold_in(jax.random.fold_in(key_of[3], part), 71), part),
        "old_values": jnp.clip(jnp.exp(jax.random.uniform(part_splits[2], (2, K), jnp.float32, math.log(1.0), math.log(4.0))), 1.0, 4.0),
    }


FULL_PRECISION = lax.Precision.HIGHEST

def cholesky_pair(matrix):
    order = matrix.shape[0]
    positions = jnp.arange(order, dtype=jnp.int32)

    def row_step(row, carry):
        lower, inverse = carry
        column = lax.dynamic_slice_in_dim(matrix, row, 1, 1)[:, 0]
        partial_row = jnp.dot(inverse, column, precision=FULL_PRECISION)
        diag_entry = lax.dynamic_slice_in_dim(column, row, 1, 0)[0]
        pivot = jnp.sqrt(diag_entry - jnp.sum(partial_row * partial_row))
        unit = (positions == row).astype(matrix.dtype)
        lower_row = partial_row + pivot * unit
        inverse_row = (unit - jnp.dot(partial_row, inverse, precision=FULL_PRECISION)) / pivot
        lower = lax.dynamic_update_slice_in_dim(lower, lower_row[None], row, 0)
        inverse = lax.dynamic_update_slice_in_dim(inverse, inverse_row[None], row, 0)
        return (lower, inverse)
    return lax.fori_loop(0, order, row_step, (jnp.zeros_like(matrix), jnp.zeros_like(matrix)))

def latitude_cosines(row_place, total_rows):
    return jnp.cos(((row_place + 0.5) / total_rows - 0.5) * (jnp.pi / 2.0))

def curl_and_divergence(wind_snaps, cosines):
    east_wind = wind_snaps[0]
    north_wind = wind_snaps[1]

    def lon_diff(values):
        return jnp.roll(values, -1, axis=1) - jnp.roll(values, 1, axis=1)

    def lat_diff(values):
        padded = jnp.pad(values * cosines, ((0, 0), (0, 0), (1, 1)))
        return padded[:, :, 2:] - padded[:, :, :-2]
    twice_cos = 2.0 * cosines
    vorticity = (lon_diff(north_wind) - lat_diff(east_wind)) / twice_cos
    divergence = (lon_diff(east_wind) + lat_diff(north_wind)) / twice_cos
    return jnp.stack([vorticity, divergence])

def project_one(gram_uu, gram_ua):
    factor_low, low_inverse = cholesky_pair(gram_uu)
    projected = jnp.dot(low_inverse, gram_ua, precision=FULL_PRECISION)
    lifted = jnp.dot(low_inverse.T, projected, precision=FULL_PRECISION)
    return (low_inverse, projected, lifted)

def upper_pair(gram):
    lower, inverse = cholesky_pair(gram)
    return (lower.T, inverse.T)

def rotate_one(low_inverse, projected, factor_up, up_inverse, values):
    rank_count = values.shape[0]
    snap_count = factor_up.shape[0]
    top_rows = jnp.concatenate([jnp.diag(values), projected], axis=1)
    bottom_rows = jnp.concatenate([jnp.zeros((snap_count, rank_count), jnp.float32), factor_up], axis=1)
    joint_matrix = jnp.concatenate([top_rows, bottom_rows], axis=0)
    square = jnp.dot(joint_matrix, joint_matrix.T, precision=FULL_PRECISION)
    subspace = jnp.eye(rank_count + snap_count, rank_count, dtype=jnp.float32)
    for sweep in range(ITERS):
        applied = jnp.dot(square, subspace, precision=FULL_PRECISION)
        inner = jnp.dot(applied.T, applied, precision=FULL_PRECISION)
        chol_low, chol_inverse = cholesky_pair(inner)
        subspace = jnp.dot(applied, chol_inverse.T, precision=FULL_PRECISION)
    energy = lax.optimization_barrier(jnp.sum(subspace * jnp.dot(square, subspace, precision=FULL_PRECISION), axis=0))
    new_values = jnp.sqrt(energy)
    mix_old = jnp.dot(low_inverse.T, subspace[:rank_count], precision=FULL_PRECISION).T
    mix_new = jnp.dot(up_inverse, subspace[rank_count:], precision=FULL_PRECISION).T
    return (mix_old, mix_new, new_values)

def reference(wind_snaps, old_basis, old_values):
    cell_count = NLON * NLAT
    cosines = latitude_cosines(jnp.arange(NLAT, dtype=jnp.float32), NLAT)
    fields = curl_and_divergence(wind_snaps, cosines).reshape(2, S, cell_count)
    basis_rows = old_basis.reshape(2, K, cell_count)
    gram_uu = jnp.einsum('fkc,fjc->fkj', basis_rows, basis_rows, precision=FULL_PRECISION) / cell_count
    gram_ua = jnp.einsum('fkc,fsc->fks', basis_rows, fields, precision=FULL_PRECISION) / cell_count
    low_inverse, projected, lifted = jax.vmap(project_one)(gram_uu, gram_ua)
    residual = fields - jnp.einsum('fks,fkc->fsc', lifted, basis_rows, precision=FULL_PRECISION)
    gram_rr = jnp.einsum('fsc,ftc->fst', residual, residual, precision=FULL_PRECISION) / cell_count
    factor_up, up_inverse = jax.vmap(upper_pair)(gram_rr)
    mix_old, mix_new, new_values = jax.vmap(rotate_one)(low_inverse, projected, factor_up, up_inverse, old_values)
    new_basis = jnp.einsum('fkj,fjc->fkc', mix_old, basis_rows, precision=FULL_PRECISION)
    new_basis = new_basis + jnp.einsum('fks,fsc->fkc', mix_new, residual, precision=FULL_PRECISION)
    return (new_basis.reshape(2, K, NLON, NLAT), new_values)
```

```python
import functools
import numpy as np
import jax
import jax.numpy as jnp
from jax import lax
from jax.experimental import pallas as pl
from jax.experimental.pallas import tpu as pltpu
from jax.sharding import PartitionSpec as P

ITERS = 2
LANES = 128
EXACT = lax.Precision.HIGHEST


def mm(a, b):
    return lax.dot_general(
        a, b, (((1,), (0,)), ((), ())), precision=EXACT, preferred_element_type=jnp.float32
    )


def mm_nt(a, b):
    return lax.dot_general(
        a, b, (((1,), (1,)), ((), ())), precision=EXACT, preferred_element_type=jnp.float32
    )


def mm_tn(a, b):
    return lax.dot_general(
        a, b, (((0,), (0,)), ((), ())), precision=EXACT, preferred_element_type=jnp.float32
    )


def lane_ids(rows):
    return lax.broadcasted_iota(jnp.int32, (rows, LANES), 1)


def row_ids(rows):
    return lax.broadcasted_iota(jnp.int32, (rows, LANES), 0)


def rows_to(value, rows):
    return jnp.concatenate([value, jnp.zeros((rows - value.shape[0], LANES), jnp.float32)], axis=0)


def eliminate(systems, first_lane):
    order = systems[0][0].shape[0]
    sub = row_ids(8)
    blocks = [
        [[chunk[8 * t : 8 * t + 8] for t in range(order // 8)] for chunk in system]
        for system in systems
    ]
    results = [[[] for _ in system] for system in systems]
    for p in range(order // 8):
        for chunks, done in zip(blocks, results):
            lane = first_lane + 8 * p
            cols = [
                [
                    jnp.broadcast_to(chunks[0][t][:, lane + j : lane + j + 1], (8, LANES))
                    for t in range(p, order // 8)
                ]
                for j in range(8)
            ]
            head = [cols[j][0] for j in range(8)]
            rows = [chunk[p] for chunk in chunks]
            factor = [jnp.zeros((8, LANES), jnp.float32) for _ in chunks]
            for j in range(8):
                col = head[j]
                pivot = jnp.broadcast_to(col[j : j + 1], (8, LANES))
                inverse = 1.0 / pivot
                here = sub == j
                root = lax.rsqrt(pivot)
                root = root * (1.5 - 0.5 * pivot * root * root)
                for jj in range(j + 1, 8):
                    scaled = jnp.broadcast_to(head[jj][j : j + 1], (8, LANES)) * inverse
                    head[jj] = jnp.where(here, scaled, head[jj] - col * scaled)
                for i in range(len(rows)):
                    top = jnp.broadcast_to(rows[i][j : j + 1], (8, LANES))
                    factor[i] = jnp.where(here, top * root, factor[i])
                    scaled = top * inverse
                    rows[i] = jnp.where(here, scaled, rows[i] - col * scaled)
            for i in range(len(chunks)):
                done[i].append(factor[i])
            for i, chunk in enumerate(chunks):
                for j in range(8):
                    top = jnp.broadcast_to(rows[i][j : j + 1], (8, LANES))
                    for t in range(p + 1, order // 8):
                        chunk[t] = chunk[t] - cols[j][t - p] * top
    return [[jnp.concatenate(done, axis=0) for done in result] for result in results]


def small_problem(packed, values, rank, snaps):
    both = rank + snaps
    lanes = lane_ids(rank)
    rows = row_ids(rank)
    snap_lanes = (lanes >= rank) & (lanes < both)
    unit = jnp.where(lanes == rows, 1.0, 0.0).astype(jnp.float32)
    first = eliminate([[w, unit] for w in packed], 0)
    fields = range(len(packed))
    projected = [jnp.where(snap_lanes, first[f][0], 0.0) for f in fields]
    low_inverse = [first[f][1] for f in fields]
    s_lanes = lane_ids(snaps)
    s_rows = row_ids(snaps)
    s_unit = jnp.where(s_lanes == s_rows + rank, 1.0, 0.0).astype(jnp.float32)
    s_mask = (s_lanes >= rank) & (s_lanes < both)
    systems = []
    for f in fields:
        aa = pltpu.roll(packed[f][:snaps], LANES - snaps, 1)
        shared = mm_tn(projected[f], projected[f])[rank:both]
        systems.append([jnp.where(s_mask, aa - shared, 0.0), s_unit])
    second = eliminate(systems, rank)
    top, joint, square, low_all = [], [], [], []
    for f in fields:
        factor_up = jnp.where(s_lanes >= s_rows + rank, second[f][0], 0.0)
        up_inverse = second[f][1]
        top.append(jnp.where(lanes == rows, values[f], projected[f]))
        joint.append(rows_to(jnp.concatenate([top[f], factor_up], axis=0), LANES))
        lifted = mm_tn(projected[f], low_inverse[f])
        mixed = up_inverse - mm(up_inverse, lifted)
        low_all.append(rows_to(jnp.concatenate([low_inverse[f], mixed], axis=0), LANES))
    applied = [mm_nt(top[f], joint[f]) for f in fields]
    square = [mm_nt(joint[f], joint[f]) for f in fields]
    for sweep in range(ITERS):
        systems = [[mm_nt(applied[f], rows_to(applied[f], LANES)), applied[f]] for f in fields]
        subspace = [result[1] for result in eliminate(systems, 0)]
        if sweep < ITERS - 1:
            applied = [mm(subspace[f], square[f]) for f in fields]
    coefficients = [mm(subspace[f], low_all[f]) for f in fields]
    stretched = [mm(subspace[f], joint[f]) for f in fields]
    ones = jnp.ones((8, LANES), jnp.float32)
    energy = [mm_nt(ones, stretched[f] * stretched[f]) for f in fields]
    return coefficients, [jnp.sqrt(e[:1]) for e in energy]


def update_kernel(lons, packed_ref, basis_ref, fields_ref, values_ref, out_ref, new_values_ref):
    rank = values_ref.shape[1]
    snaps = fields_ref.shape[1]
    packed = [packed_ref[f] for f in range(2)]
    values = [values_ref[f : f + 1, :] for f in range(2)]
    values = [jnp.concatenate([v, jnp.zeros((1, LANES - rank), jnp.float32)], axis=1) for v in values]
    coefficients, new_values = small_problem(packed, values, rank, snaps)
    pad = jnp.zeros((LANES - rank - snaps, lons * LANES), jnp.float32)
    for f in range(2):
        basis = jnp.concatenate(
            [basis_ref[f, pl.ds(i, rank, stride=lons), :] for i in range(lons)], axis=1
        )
        cells = jnp.concatenate([basis, fields_ref[f], pad], axis=0)
        result = mm(coefficients[f], cells)
        for i in range(lons):
            out_ref[f, pl.ds(i, rank, stride=lons), :] = result[:, i * LANES : (i + 1) * LANES]
        new_values_ref[f : f + 1, :] = new_values[f]


def gram_kernel(
    lons, rank, snaps, count, lat_count, cell_count, reduce_here,
    wind_ref, basis_ref, cos_ref,
    fields_ref, sum_ref,
    send_low, send_high, send_lat, got_low, got_high, got_lat,
    local, parts, own, halo_send, halo_got, part_send, part_got, own_send, own_got,
):
    lon, lat = lax.axis_index("lon"), lax.axis_index("lat")
    size = count * lat_count
    me = lon * lat_count + lat

    def place(index):
        return {"lon": lax.div(index, lat_count), "lat": lax.rem(index, lat_count)}

    up = {"lon": lax.rem(lon + 1, count), "lat": lat}
    down = {"lon": lax.rem(lon + count - 1, count), "lat": lat}
    mate = {"lon": lon, "lat": 1 - lat}
    if reduce_here:
        peers = [place(lax.rem(me + o, size)) for o in range(1, size)]
    else:
        peers = [up, down, mate]
    barrier = pltpu.get_barrier_semaphore()
    for peer in peers:
        pl.semaphore_signal(barrier, inc=1, device_id=peer, device_id_type=pl.DeviceIdType.MESH)

    def wind(c, i):
        return wind_ref[c, pl.ds(i, snaps, stride=lons), :]

    lane = lane_ids(snaps)
    first_lat = lat == 0
    cosines = jnp.where(first_lat, cos_ref[0:1], cos_ref[1:2])
    half_over = jnp.where(first_lat, cos_ref[2:3], cos_ref[3:4])
    edge = jnp.zeros((snaps, LANES), jnp.float32)
    winds = [[wind(c, i) for i in range(lons)] for c in range(2)]
    weighted = [[w * cosines for w in line] for line in winds]
    for c in range(2):
        send_low[c] = winds[c][0]
        send_high[c] = winds[c][lons - 1]
        for i in range(lons):
            w = weighted[c][i]
            last = jnp.broadcast_to(w[:, LANES - 1 :], (snaps, LANES))
            first = jnp.broadcast_to(w[:, :1], (snaps, LANES))
            edge = jnp.where(lane == c * lons + i, jnp.where(first_lat, last, first), edge)
    send_lat[...] = edge
    pl.semaphore_wait(barrier, len(peers))

    def send(src, dst, sem, got, peer):
        copy = pltpu.make_async_remote_copy(
            src_ref=src, dst_ref=dst, send_sem=sem, recv_sem=got,
            device_id=peer, device_id_type=pl.DeviceIdType.MESH,
        )
        copy.start()
        return copy

    halo = [
        send(send_low, got_high, halo_send.at[0], halo_got.at[0], down),
        send(send_high, got_low, halo_send.at[1], halo_got.at[1], up),
        send(send_lat, got_lat, halo_send.at[2], halo_got.at[2], mate),
    ]
    bases = [
        jnp.concatenate([basis_ref[f, pl.ds(i, rank, stride=lons), :] for i in range(lons)], axis=1)
        for f in range(2)
    ]
    grams = [mm_nt(b, jnp.concatenate([b, jnp.zeros_like(b)], axis=0)) for b in bases]
    for copy in halo:
        copy.wait()
    side = got_lat[...]
    before = [got_low[c] for c in range(2)]
    after = [got_high[c] for c in range(2)]

    def lon_diff(c, i):
        nxt = winds[c][i + 1] if i < lons - 1 else after[c]
        prv = winds[c][i - 1] if i > 0 else before[c]
        return nxt - prv

    def lat_diff(c, i):
        w = weighted[c][i]
        k = c * lons + i
        outer = jnp.broadcast_to(side[:, k : k + 1], (snaps, LANES))
        nxt = pltpu.roll(w, LANES - 1, 1)
        prv = pltpu.roll(w, 1, 1)
        nxt = jnp.where(lane == LANES - 1, jnp.where(first_lat, outer, 0.0), nxt)
        prv = jnp.where(lane == 0, jnp.where(first_lat, 0.0, outer), prv)
        return nxt - prv

    for f in range(2):
        parts_of = []
        for i in range(lons):
            if f == 0:
                value = lon_diff(1, i) - lat_diff(0, i)
            else:
                value = lon_diff(0, i) + lat_diff(1, i)
            parts_of.append(value * half_over)
        field = jnp.concatenate(parts_of, axis=1)
        fields_ref[f] = field
        gap = jnp.zeros((rank, lons * LANES), jnp.float32)
        tail = jnp.zeros((LANES - rank - snaps, lons * LANES), jnp.float32)
        cross = mm_nt(bases[f], jnp.concatenate([gap, field, tail], axis=0))
        inner = mm_nt(field, jnp.concatenate([gap, tail, field], axis=0))
        packed = (grams[f] + cross + rows_to(inner, rank)) * (1.0 / cell_count)
        for t in range(rank // 8):
            if reduce_here:
                local[f * (rank // 8) + t] = packed[8 * t : 8 * t + 8]
            else:
                sum_ref[f * (rank // 8) + t] = packed[8 * t : 8 * t + 8]
    if not reduce_here:
        return
    copies = []
    for o in range(1, size):
        there = lax.rem(me + o, size)
        copies.append(
            send(local.at[there], parts.at[o - 1], part_send.at[o - 1], part_got.at[o - 1], peers[o - 1])
        )
    total = local[me]
    for o in range(1, size):
        copies[o - 1].wait_recv()
        total = total + parts[o - 1]
    own[...] = total
    sum_ref[me] = total
    gathers = []
    for o in range(1, size):
        gathers.append(
            send(own, sum_ref.at[me], own_send.at[o - 1], own_got.at[o - 1], peers[o - 1])
        )
    for o in range(1, size):
        copies[o - 1].wait_send()
    for o in range(1, size):
        source = lax.rem(me + size - o, size)
        pltpu.make_async_remote_copy(
            src_ref=own, dst_ref=sum_ref.at[source], send_sem=own_send.at[o - 1],
            recv_sem=own_got.at[o - 1], device_id=peers[o - 1], device_id_type=pl.DeviceIdType.MESH,
        ).wait_recv()
    for copy in gathers:
        copy.wait_send()


def per_device(wind_snaps, old_basis, old_values):
    snaps, rank = wind_snaps.shape[1], old_basis.shape[1]
    lons, lats = wind_snaps.shape[2:]
    count, lat_count = lax.axis_size("lon"), lax.axis_size("lat")
    size = count * lat_count
    rows_all = lats * lat_count
    cell_count = lons * count * rows_all
    assert lats == LANES and lat_count == 2 and count > 2 and rank + 2 * snaps == LANES
    place = np.arange(rows_all, dtype=np.float64)
    cosines = np.cos(((place + 0.5) / rows_all - 0.5) * (np.pi / 2.0))
    table = np.concatenate([cosines, 0.5 / cosines]).reshape(4, LANES)
    table = np.concatenate([table, np.zeros((4, LANES))]).astype(np.float32)
    tiles = 2 * rank // 8
    reduce_here = size == tiles
    wind_rows = wind_snaps.reshape(2, snaps * lons, LANES)
    basis_rows = old_basis.reshape(2, rank * lons, LANES)
    vmem = pl.BlockSpec(memory_space=pltpu.VMEM)
    many = size - 1 if reduce_here else 1
    fields, packed = pl.pallas_call(
        functools.partial(
            gram_kernel, lons, rank, snaps, count, lat_count, cell_count, reduce_here
        ),
        out_shape=(
            jax.ShapeDtypeStruct((2, snaps, lons * LANES), jnp.float32),
            jax.ShapeDtypeStruct((tiles, 8, LANES), jnp.float32),
        ),
        in_specs=[vmem] * 3,
        out_specs=(vmem, vmem),
        scratch_shapes=[
            pltpu.VMEM((2, snaps, LANES), jnp.float32),
            pltpu.VMEM((2, snaps, LANES), jnp.float32),
            pltpu.VMEM((snaps, LANES), jnp.float32),
            pltpu.VMEM((2, snaps, LANES), jnp.float32),
            pltpu.VMEM((2, snaps, LANES), jnp.float32),
            pltpu.VMEM((snaps, LANES), jnp.float32),
            pltpu.VMEM((tiles, 8, LANES), jnp.float32),
            pltpu.VMEM((many, 8, LANES), jnp.float32),
            pltpu.VMEM((8, LANES), jnp.float32),
            pltpu.SemaphoreType.DMA((3,)),
            pltpu.SemaphoreType.DMA((3,)),
            pltpu.SemaphoreType.DMA((many,)),
            pltpu.SemaphoreType.DMA((many,)),
            pltpu.SemaphoreType.DMA((many,)),
            pltpu.SemaphoreType.DMA((many,)),
        ],
        compiler_params=pltpu.CompilerParams(
            collective_id=0, has_side_effects=True, vmem_limit_bytes=16 * 2**20
        ),
        name="gram",
    )(wind_rows, basis_rows, jnp.asarray(table))
    if not reduce_here:
        packed = lax.psum(packed, ("lon", "lat"))
    new_basis, new_values = pl.pallas_call(
        functools.partial(update_kernel, lons),
        out_shape=(
            jax.ShapeDtypeStruct((2, rank * lons, LANES), jnp.float32),
            jax.ShapeDtypeStruct((2, rank), jnp.float32),
        ),
        in_specs=[vmem] * 4,
        out_specs=(vmem, vmem),
        compiler_params=pltpu.CompilerParams(vmem_limit_bytes=24 * 2**20),
        name="update",
    )(packed.reshape(2, rank, LANES), basis_rows, fields, old_values)
    return new_basis.reshape(2, rank, lons, LANES), new_values


def solution(mesh):
    placed = (P("level", None, "lon", "lat"), P("level", None, "lon", "lat"), P("level", None))
    return jax.shard_map(
        per_device,
        mesh=mesh,
        in_specs=placed,
        out_specs=(P("level", None, "lon", "lat"), P("level", None)),
        check_vma=False,
    )
```

```python
import functools
import numpy as np
import jax
import jax.numpy as jnp
from jax import lax
from jax.experimental import pallas as pl
from jax.experimental.pallas import tpu as pltpu
from jax.sharding import PartitionSpec as P

ITERS = 2
LANES = 128
EXACT = lax.Precision.HIGHEST


def mm(a, b):
    return lax.dot_general(
        a, b, (((1,), (0,)), ((), ())), precision=EXACT, preferred_element_type=jnp.float32
    )


def mm_nt(a, b):
    return lax.dot_general(
        a, b, (((1,), (1,)), ((), ())), precision=EXACT, preferred_element_type=jnp.float32
    )


def mm_tn(a, b):
    return lax.dot_general(
        a, b, (((0,), (0,)), ((), ())), precision=EXACT, preferred_element_type=jnp.float32
    )


def lane_ids(rows):
    return lax.broadcasted_iota(jnp.int32, (rows, LANES), 1)


def row_ids(rows):
    return lax.broadcasted_iota(jnp.int32, (rows, LANES), 0)


def rows_to(value, rows):
    return jnp.concatenate([value, jnp.zeros((rows - value.shape[0], LANES), jnp.float32)], axis=0)


def eliminate(systems, first_lane):
    order = systems[0][0].shape[0]
    sub = row_ids(8)
    blocks = [
        [[chunk[8 * t : 8 * t + 8] for t in range(order // 8)] for chunk in system]
        for system in systems
    ]
    results = [[[] for _ in system] for system in systems]
    for p in range(order // 8):
        for chunks, done in zip(blocks, results):
            lane = first_lane + 8 * p
            cols = [
                [
                    jnp.broadcast_to(chunks[0][t][:, lane + j : lane + j + 1], (8, LANES))
                    for t in range(p, order // 8)
                ]
                for j in range(8)
            ]
            head = [cols[j][0] for j in range(8)]
            rows = [chunk[p] for chunk in chunks]
            factor = [jnp.zeros((8, LANES), jnp.float32) for _ in chunks]
            for j in range(8):
                col = head[j]
                pivot = jnp.broadcast_to(col[j : j + 1], (8, LANES))
                inverse = 1.0 / pivot
                here = sub == j
                root = lax.rsqrt(pivot)
                root = root * (1.5 - 0.5 * pivot * root * root)
                for jj in range(j + 1, 8):
                    scaled = jnp.broadcast_to(head[jj][j : j + 1], (8, LANES)) * inverse
                    head[jj] = jnp.where(here, scaled, head[jj] - col * scaled)
                for i in range(len(rows)):
                    top = jnp.broadcast_to(rows[i][j : j + 1], (8, LANES))
                    factor[i] = jnp.where(here, top * root, factor[i])
                    scaled = top * inverse
                    rows[i] = jnp.where(here, scaled, rows[i] - col * scaled)
            for i in range(len(chunks)):
                done[i].append(factor[i])
            for i, chunk in enumerate(chunks):
                for j in range(8):
                    top = jnp.broadcast_to(rows[i][j : j + 1], (8, LANES))
                    for t in range(p + 1, order // 8):
                        chunk[t] = chunk[t] - cols[j][t - p] * top
    return [[jnp.concatenate(done, axis=0) for done in result] for result in results]


def small_problem(packed, values, rank, snaps):
    both = rank + snaps
    lanes = lane_ids(rank)
    rows = row_ids(rank)
    snap_lanes = (lanes >= rank) & (lanes < both)
    unit = jnp.where(lanes == rows, 1.0, 0.0).astype(jnp.float32)
    first = eliminate([[w, unit] for w in packed], 0)
    fields = range(len(packed))
    projected = [jnp.where(snap_lanes, first[f][0], 0.0) for f in fields]
    low_inverse = [first[f][1] for f in fields]
    s_lanes = lane_ids(snaps)
    s_rows = row_ids(snaps)
    s_unit = jnp.where(s_lanes == s_rows + rank, 1.0, 0.0).astype(jnp.float32)
    s_mask = (s_lanes >= rank) & (s_lanes < both)
    systems = []
    for f in fields:
        aa = pltpu.roll(packed[f][:snaps], LANES - snaps, 1)
        shared = mm_tn(projected[f], projected[f])[rank:both]
        systems.append([jnp.where(s_mask, aa - shared, 0.0), s_unit])
    second = eliminate(systems, rank)
    top, joint, square, low_all = [], [], [], []
    for f in fields:
        factor_up = jnp.where(s_lanes >= s_rows + rank, second[f][0], 0.0)
        up_inverse = second[f][1]
        top.append(jnp.where(lanes == rows, values[f], projected[f]))
        joint.append(rows_to(jnp.concatenate([top[f], factor_up], axis=0), LANES))
        lifted = mm_tn(projected[f], low_inverse[f])
        mixed = up_inverse - mm(up_inverse, lifted)
        low_all.append(rows_to(jnp.concatenate([low_inverse[f], mixed], axis=0), LANES))
    applied = [mm_nt(top[f], joint[f]) for f in fields]
    square = [mm_nt(joint[f], joint[f]) for f in fields]
    for sweep in range(ITERS):
        systems = [[mm_nt(applied[f], rows_to(applied[f], LANES)), applied[f]] for f in fields]
        subspace = [result[1] for result in eliminate(systems, 0)]
        if sweep < ITERS - 1:
            applied = [mm(subspace[f], square[f]) for f in fields]
    coefficients = [mm(subspace[f], low_all[f]) for f in fields]
    stretched = [mm(subspace[f], joint[f]) for f in fields]
    ones = jnp.ones((8, LANES), jnp.float32)
    energy = [mm_nt(ones, stretched[f] * stretched[f]) for f in fields]
    return coefficients, [jnp.sqrt(e[:1]) for e in energy]


def update(lons, packed, basis_ref, fields_ref, values_ref, finish, new_values_ref):
    rank = values_ref.shape[1]
    snaps = fields_ref.shape[1]
    values = [values_ref[f : f + 1, :] for f in range(2)]
    values = [jnp.concatenate([v, jnp.zeros((1, LANES - rank), jnp.float32)], axis=1) for v in values]
    coefficients, new_values = small_problem(packed, values, rank, snaps)
    pad = jnp.zeros((LANES - rank - snaps, lons * LANES), jnp.float32)
    for f in range(2):
        new_values_ref[f : f + 1, :] = new_values[f]
        basis = jnp.concatenate(
            [basis_ref[f, pl.ds(i, rank, stride=lons), :] for i in range(lons)], axis=1
        )
        cells = jnp.concatenate([basis, fields_ref[f], pad], axis=0)
        finish(f, mm(coefficients[f], cells))


def update_kernel(lons, packed_ref, basis_ref, fields_ref, values_ref, out_ref, new_values_ref):
    rank = values_ref.shape[1]

    def finish(f, result):
        for i in range(lons):
            out_ref[f, pl.ds(i, rank, stride=lons), :] = result[:, i * LANES : (i + 1) * LANES]

    packed = [packed_ref[f] for f in range(2)]
    update(lons, packed, basis_ref, fields_ref, values_ref, finish, new_values_ref)


def gram_part(
    lons, rank, snaps, count, lat_count, cell_count, reduce_here,
    wind_hbm, basis_hbm, cos_hbm, values_hbm,
    fields_ref, sum_ref, values_ref,
    wind_ref, basis_ref, cos_ref, load_sem, send_low, send_high, send_lat, got_low, got_high, got_lat,
    local, parts, by_layer, halo_send, halo_got, sends, gots,
):
    lon, lat = lax.axis_index("lon"), lax.axis_index("lat")
    size = count * lat_count
    me = lon * lat_count + lat

    def place(index):
        return {"lon": lax.div(index, lat_count), "lat": lax.rem(index, lat_count)}

    up = {"lon": lax.rem(lon + 1, count), "lat": lat}
    down = {"lon": lax.rem(lon + count - 1, count), "lat": lat}
    mate = {"lon": lon, "lat": 1 - lat}
    if reduce_here:
        peers = [place(lax.rem(me + o, size)) for o in range(1, size)]
    else:
        peers = [up, down, mate]
    barrier = pltpu.get_barrier_semaphore()
    for peer in peers:
        pl.semaphore_signal(barrier, inc=1, device_id=peer, device_id_type=pl.DeviceIdType.MESH)

    loads = [
        pltpu.make_async_copy(src, dst, load_sem.at[k])
        for k, (src, dst) in enumerate(
            [(wind_hbm, wind_ref), (cos_hbm, cos_ref), (basis_hbm, basis_ref), (values_hbm, values_ref)]
        )
    ]
    for load in loads:
        load.start()
    loads[0].wait()
    loads[1].wait()

    def wind(c, i):
        return wind_ref[c, pl.ds(i, snaps, stride=lons), :]

    lane = lane_ids(snaps)
    first_lat = lat == 0
    cosines = jnp.where(first_lat, cos_ref[0:1], cos_ref[1:2])
    half_over = jnp.where(first_lat, cos_ref[2:3], cos_ref[3:4])
    edge = jnp.zeros((snaps, LANES), jnp.float32)
    winds = [[wind(c, i) for i in range(lons)] for c in range(2)]
    weighted = [[w * cosines for w in line] for line in winds]
    for c in range(2):
        send_low[c] = winds[c][0]
        send_high[c] = winds[c][lons - 1]
        for i in range(lons):
            w = weighted[c][i]
            last = jnp.broadcast_to(w[:, LANES - 1 :], (snaps, LANES))
            first = jnp.broadcast_to(w[:, :1], (snaps, LANES))
            edge = jnp.where(lane == c * lons + i, jnp.where(first_lat, last, first), edge)
    send_lat[...] = edge
    pl.semaphore_wait(barrier, len(peers))

    def send(src, dst, sem, got, peer):
        copy = pltpu.make_async_remote_copy(
            src_ref=src, dst_ref=dst, send_sem=sem, recv_sem=got,
            device_id=peer, device_id_type=pl.DeviceIdType.MESH,
        )
        copy.start()
        return copy

    halo = [
        send(send_low, got_high, halo_send.at[0], halo_got.at[0], down),
        send(send_high, got_low, halo_send.at[1], halo_got.at[1], up),
        send(send_lat, got_lat, halo_send.at[2], halo_got.at[2], mate),
    ]
    loads[2].wait()
    bases = [
        jnp.concatenate([basis_ref[f, pl.ds(i, rank, stride=lons), :] for i in range(lons)], axis=1)
        for f in range(2)
    ]
    grams = [mm_nt(b, jnp.concatenate([b, jnp.zeros_like(b)], axis=0)) for b in bases]
    for copy in halo:
        copy.wait()
    side = got_lat[...]
    before = [got_low[c] for c in range(2)]
    after = [got_high[c] for c in range(2)]

    def lon_diff(c, i):
        nxt = winds[c][i + 1] if i < lons - 1 else after[c]
        prv = winds[c][i - 1] if i > 0 else before[c]
        return nxt - prv

    def lat_diff(c, i):
        w = weighted[c][i]
        k = c * lons + i
        outer = jnp.broadcast_to(side[:, k : k + 1], (snaps, LANES))
        nxt = pltpu.roll(w, LANES - 1, 1)
        prv = pltpu.roll(w, 1, 1)
        nxt = jnp.where(lane == LANES - 1, jnp.where(first_lat, outer, 0.0), nxt)
        prv = jnp.where(lane == 0, jnp.where(first_lat, 0.0, outer), prv)
        return nxt - prv

    for f in range(2):
        parts_of = []
        for i in range(lons):
            if f == 0:
                value = lon_diff(1, i) - lat_diff(0, i)
            else:
                value = lon_diff(0, i) + lat_diff(1, i)
            parts_of.append(value * half_over)
        field = jnp.concatenate(parts_of, axis=1)
        fields_ref[f] = field
        gap = jnp.zeros((rank, lons * LANES), jnp.float32)
        tail = jnp.zeros((LANES - rank - snaps, lons * LANES), jnp.float32)
        right = mm_nt(jnp.concatenate([bases[f], field], axis=0), jnp.concatenate([gap, field, tail], axis=0))
        inner = pltpu.roll(right[rank:], snaps, 1)
        packed = (grams[f] + right[:rank] + rows_to(inner, rank)) * (1.0 / cell_count)
        half = rank // 2
        for t in range(2):
            target = local if reduce_here else sum_ref
            target[2 * f + t] = packed[half * t : half * t + half]
    loads[3].wait()
    if not reduce_here:
        return
    plane = lax.rem(lon, 2) * lat_count + lat
    layer = lax.div(lon, 2)
    layers = count // 2

    def member(index):
        return {"lon": layer * 2 + lax.div(index, 2), "lat": lax.rem(index, 2)}

    def across(index):
        return {"lon": index * 2 + lax.rem(lon, 2), "lat": lat}

    copies = []
    for o in range(1, 4):
        there = lax.rem(plane + o, 4)
        copies.append(
            send(local.at[there], parts.at[o - 1], sends.at[o - 1], gots.at[o - 1], member(there))
        )
    total = local[plane]
    for o in range(1, 4):
        copies[o - 1].wait_recv()
        total = total + parts[o - 1]
    by_layer[layer] = total
    crossing = []
    for o in range(1, layers):
        there = lax.rem(layer + o, layers)
        k = 2 + o
        crossing.append(
            send(by_layer.at[layer], by_layer.at[layer], sends.at[k], gots.at[k], across(there))
        )
    for o in range(1, layers):
        there = lax.rem(layer + layers - o, layers)
        k = 2 + o
        pltpu.make_async_remote_copy(
            src_ref=by_layer.at[layer], dst_ref=by_layer.at[there], send_sem=sends.at[k],
            recv_sem=gots.at[k], device_id=across(there), device_id_type=pl.DeviceIdType.MESH,
        ).wait_recv()
    total = by_layer[0]
    for z in range(1, layers):
        total = total + by_layer[z]
    sum_ref[plane] = total
    gathers = []
    for o in range(1, 4):
        there = lax.rem(plane + o, 4)
        k = 1 + layers + o
        gathers.append(
            send(sum_ref.at[plane], sum_ref.at[plane], sends.at[k], gots.at[k], member(there))
        )
    for o in range(1, 4):
        there = lax.rem(plane + 4 - o, 4)
        k = 1 + layers + o
        pltpu.make_async_remote_copy(
            src_ref=sum_ref.at[plane], dst_ref=sum_ref.at[there], send_sem=sends.at[k],
            recv_sem=gots.at[k], device_id=member(there), device_id_type=pl.DeviceIdType.MESH,
        ).wait_recv()
    for copy in copies + crossing + gathers:
        copy.wait_send()


def gram_kernel(*args):
    gram_part(*args)


def whole_kernel(*args):
    config, rest = args[:7], args[7:]
    inputs, (out_hbm, new_values_ref), scratch = rest[:4], rest[4:6], rest[6:]
    fields_ref, sum_ref, values_ref, staged, out_sem = scratch[:5]
    gram_part(*config, *inputs, fields_ref, sum_ref, values_ref, *scratch[5:])
    basis_ref = scratch[6]
    lons, rank = config[:2]
    outgoing = []

    def finish(f, result):
        for i in range(lons):
            staged[f, pl.ds(i, rank, stride=lons), :] = result[:, i * LANES : (i + 1) * LANES]
        copy = pltpu.make_async_copy(staged.at[f], out_hbm.at[f], out_sem.at[f])
        copy.start()
        outgoing.append(copy)

    packed = [jnp.concatenate([sum_ref[2 * f], sum_ref[2 * f + 1]], axis=0) for f in range(2)]
    update(lons, packed, basis_ref, fields_ref, values_ref, finish, new_values_ref)
    for copy in outgoing:
        copy.wait()


def per_device(wind_snaps, old_basis, old_values):
    snaps, rank = wind_snaps.shape[1], old_basis.shape[1]
    lons, lats = wind_snaps.shape[2:]
    count, lat_count = lax.axis_size("lon"), lax.axis_size("lat")
    size = count * lat_count
    rows_all = lats * lat_count
    cell_count = lons * count * rows_all
    assert lats == LANES and lat_count == 2 and count > 2 and rank + 2 * snaps == LANES
    place = np.arange(rows_all, dtype=np.float64)
    cosines = np.cos(((place + 0.5) / rows_all - 0.5) * (np.pi / 2.0))
    table = np.concatenate([cosines, 0.5 / cosines]).reshape(4, LANES)
    table = np.concatenate([table, np.zeros((4, LANES))]).astype(np.float32)
    reduce_here = size <= 16 and count % 2 == 0
    wind_rows = wind_snaps.reshape(2, snaps * lons, LANES)
    basis_rows = old_basis.reshape(2, rank * lons, LANES)
    vmem = pl.BlockSpec(memory_space=pltpu.VMEM)
    hbm = pl.BlockSpec(memory_space=pltpu.HBM)
    scratch = [
        pltpu.VMEM((2, snaps * lons, LANES), jnp.float32),
        pltpu.VMEM((2, rank * lons, LANES), jnp.float32),
        pltpu.VMEM((8, LANES), jnp.float32),
        pltpu.SemaphoreType.DMA((4,)),
        pltpu.VMEM((2, snaps, LANES), jnp.float32),
        pltpu.VMEM((2, snaps, LANES), jnp.float32),
        pltpu.VMEM((snaps, LANES), jnp.float32),
        pltpu.VMEM((2, snaps, LANES), jnp.float32),
        pltpu.VMEM((2, snaps, LANES), jnp.float32),
        pltpu.VMEM((snaps, LANES), jnp.float32),
        pltpu.VMEM((4, rank // 2, LANES), jnp.float32),
        pltpu.VMEM((3, rank // 2, LANES), jnp.float32),
        pltpu.VMEM((count // 2, rank // 2, LANES), jnp.float32),
        pltpu.SemaphoreType.DMA((3,)),
        pltpu.SemaphoreType.DMA((3,)),
        pltpu.SemaphoreType.DMA((5 + count // 2,)),
        pltpu.SemaphoreType.DMA((5 + count // 2,)),
    ]
    gram_out = [(2, snaps, lons * LANES), (4, rank // 2, LANES), (2, rank)]
    out_shape = (
        jax.ShapeDtypeStruct((2, rank * lons, LANES), jnp.float32),
        jax.ShapeDtypeStruct((2, rank), jnp.float32),
    )
    config = (lons, rank, snaps, count, lat_count, cell_count, reduce_here)
    inputs = (wind_rows, basis_rows, jnp.asarray(table), old_values)
    params = pltpu.CompilerParams(
        collective_id=0, has_side_effects=True, vmem_limit_bytes=62 * 2**20
    )
    if reduce_here:
        new_basis, new_values = pl.pallas_call(
            functools.partial(whole_kernel, *config),
            out_shape=out_shape,
            in_specs=[hbm] * 4,
            out_specs=(hbm, vmem),
            scratch_shapes=[pltpu.VMEM(shape, jnp.float32) for shape in gram_out]
            + [pltpu.VMEM(out_shape[0].shape, jnp.float32), pltpu.SemaphoreType.DMA((2,))]
            + scratch,
            compiler_params=params,
            name="whole",
        )(*inputs)
        return new_basis.reshape(2, rank, lons, LANES), new_values
    fields, packed, values = pl.pallas_call(
        functools.partial(gram_kernel, *config),
        out_shape=tuple(jax.ShapeDtypeStruct(shape, jnp.float32) for shape in gram_out),
        in_specs=[hbm] * 4,
        out_specs=(vmem, vmem, vmem),
        scratch_shapes=scratch,
        compiler_params=params,
        name="gram",
    )(*inputs)
    packed = lax.psum(packed, ("lon", "lat"))
    new_basis, new_values = pl.pallas_call(
        functools.partial(update_kernel, lons),
        out_shape=out_shape,
        in_specs=[vmem] * 4,
        out_specs=(vmem, vmem),
        compiler_params=pltpu.CompilerParams(vmem_limit_bytes=24 * 2**20),
        name="update",
    )(packed.reshape(2, rank, LANES), basis_rows, fields, values)
    return new_basis.reshape(2, rank, lons, LANES), new_values


def solution(mesh):
    placed = (P("level", None, "lon", "lat"), P("level", None, "lon", "lat"), P("level", None))
    return jax.shard_map(
        per_device,
        mesh=mesh,
        in_specs=placed,
        out_specs=(P("level", None, "lon", "lat"), P("level", None)),
        check_vma=False,
    )
```
